256 devices in a mesh: island: 32 (over y, z_hi, x), fsdp: 8 (over z_lo, core).
Axes of the slice: x: 4, y: 4, z: 8 (z_hi: 2, z_lo: 4; z = z_hi * 4 + z_lo), core: 2. Of those that a mesh axis runs over, the one named last changes fastest.
Arguments:
- tokens: bfloat16 [32, 2048, 12288], P('island', 'fsdp'), may hold values from -6 to 6
- targets: bfloat16 [32, 2048, 256], P('island', 'fsdp'), may hold values from -6 to 6
- loss_mask: int32 [32, 2048], P('island', 'fsdp'), may hold values 0 or 1
- norm_gain: float32 [12288], replicated, may hold values from 0.5 to 1.5
- params: float32 [32, 12288, 256], P('island', 'fsdp'), may hold values from -0.0546875 to 0.0546875
- moment_one: float32 [32, 12288, 256], P('island', 'fsdp'), may hold values from -0.12 to 0.12
- moment_two: float32 [32, 12288, 256], P('island', 'fsdp'), may hold values from 0.0001 to 0.002
- outer_delta: float32 [32, 12288, 128], P('island', 'fsdp'), may hold values from -6 to 6
- outer_momentum: float32 [12288, 128], P('fsdp'), may hold values from -6 to 6
Outputs:
- params_new: float32 [32, 12288, 256], P('island', 'fsdp')
- momentum_new: float32 [12288, 128], P('fsdp')
- outer_update: float32 [12288, 128], P('fsdp')
The draws below stay inside these ranges and needn't reach their ends.
All inputs are finite; a program needn't handle non-finite values. No bound on the sum of `loss_mask` on one device may be relied on, other than what follows from the above.
Results may differ from the reference program's by a relative error of at most 0.0025.
Values may be sent and summed in bfloat16 or wider, within the bound.
No kernel may reach another device: no remote copies, remote signals or barrier semaphores. Data moves between devices by JAX's collectives and lax.ppermute only.
A program may use at most 128 MiB of HBM per device.

```python
import math
import jax
import jax.numpy as jnp
from jax import lax

D = 12288
HD = 256
OHD = 128
TOK_ISL = 2048
ISLANDS = 32


def set_ends(array, rng, smallest, top_value):
    shape = array.shape
    place = [jax.random.randint(jax.random.fold_in(rng, axis), (), 0, shape[axis]) for axis in range(len(shape))]
    array = array.at[tuple(place)].set(smallest)
    longest = shape.index(max(shape))
    place[longest] = (place[longest] + 1) % shape[longest]
    return array.at[tuple(place)].set(top_value)


def level_of(key, dims, split, smallest, largest):
    level = 1.0
    for axis_at, blocks in split:
        draws = jax.random.uniform(jax.random.fold_in(jax.random.fold_in(key, 6), axis_at), (blocks,), jnp.float32, smallest / len(split), largest / len(split))
        level = level * jnp.repeat(jnp.exp(draws), dims[axis_at] // blocks).reshape((-1,) + (1,) * (len(dims) - 1 - axis_at))
    return level


def normal_values(rng, dims, spread, bound, shards=(), held_as=jnp.bfloat16):
    values = spread * jax.random.normal(rng, dims, jnp.float32)
    if shards:
        values = values * level_of(rng, dims, shards, -0.22, 0.18)
    return jnp.clip(values, -bound, bound).astype(held_as)


def setup_inputs(seed: int = 0) -> dict:
    arg_keys = jax.random.split(jax.random.key(seed), 10)
    tokens = normal_values(arg_keys[0], (ISLANDS, TOK_ISL, D), 1.0, 6.0, ((0, 32), (1, 8)))
    targets = normal_values(arg_keys[1], (ISLANDS, TOK_ISL, HD), 1.0, 6.0, ((0, 32), (1, 8)))
    loss_mask = set_ends((jax.random.randint(arg_keys[2], (ISLANDS, TOK_ISL), 0, 4) < 3).astype(jnp.int32), jax.random.fold_in(arg_keys[2], 1), 0, 1)
    norm_gain = jnp.clip(1.0 + 0.1 * jax.random.normal(arg_keys[3], (D,), jnp.float32), 0.5, 1.5)
    params = normal_values(arg_keys[4], (ISLANDS, D, HD), D ** -0.5, 0.0546875, ((0, 32), (1, 8)), jnp.float32)
    moment_one = normal_values(arg_keys[5], (ISLANDS, D, HD), 0.02, 0.12, ((0, 32), (1, 8)), jnp.float32)
    moment_two = jnp.clip(jnp.exp(math.log(0.002) - 2.9957323 * jax.random.uniform(arg_keys[6], (ISLANDS, D, HD), jnp.float32) ** level_of(arg_keys[6], (ISLANDS, D, HD), ((0, 32), (1, 8)), -0.2, 0.2)), 0.0001, 0.002)
    outer_delta = normal_values(arg_keys[7], (ISLANDS, D, OHD), 1.0, 6.0, ((0, 32), (1, 8)), jnp.float32)
    outer_momentum = normal_values(arg_keys[8], (D, OHD), 1.0, 6.0, ((0, 8),), jnp.float32)
    return {"tokens": tokens, "targets": targets, "loss_mask": loss_mask, "norm_gain": norm_gain, "params": params, "moment_one": moment_one, "moment_two": moment_two, "outer_delta": outer_delta, "outer_momentum": outer_momentum}


ADAM_BETA_ONE = 0.9
ADAM_BETA_TWO = 0.95
ADAM_EPSILON = 1e-08
INNER_RATE = 0.005
WEIGHT_DECAY = 0.1
NORM_EPSILON = 1e-05
OUTER_RATE = 0.7
OUTER_MOMENTUM = 0.9
STEP_BASE = 1000

def adam_update(weights, first_moment, second_moment, gradient, count):
    first_moment = ADAM_BETA_ONE * first_moment + (1.0 - ADAM_BETA_ONE) * gradient
    second_moment = ADAM_BETA_TWO * second_moment + (1.0 - ADAM_BETA_TWO) * gradient * gradient
    first_hat = first_moment / (1.0 - ADAM_BETA_ONE ** count)
    second_hat = second_moment / (1.0 - ADAM_BETA_TWO ** count)
    weights = weights - INNER_RATE * (first_hat / (jnp.sqrt(second_hat) + ADAM_EPSILON) + WEIGHT_DECAY * weights)
    return (weights, first_moment, second_moment)

def reference(tokens, targets, loss_mask, norm_gain, params, moment_one, moment_two, outer_delta, outer_momentum):

    def one_island(pieces):
        rows_in, goal_in, mask_in, weights, first_moment, second_moment = pieces
        inputs_f = rows_in.astype(jnp.float32)
        row_scale = lax.rsqrt(lax.optimization_barrier(jnp.mean(inputs_f * inputs_f, axis=1)) + NORM_EPSILON)
        scaled = (inputs_f * norm_gain).astype(jnp.bfloat16)
        keep_rows = mask_in.astype(jnp.float32)
        goal_rows = goal_in.astype(jnp.float32)
        token_count = scaled.shape[0]
        for inner_step in range(2):
            weights_bf = weights.astype(jnp.bfloat16)
            value_rows = row_scale[:, None] * jnp.dot(scaled, weights_bf, preferred_element_type=jnp.float32)
            residual_rows = (row_scale[:, None] * keep_rows[:, None] * (value_rows - goal_rows) / token_count).astype(jnp.bfloat16)
            gradient = lax.dot_general(scaled, residual_rows, (((0,), (0,)), ((), ())), preferred_element_type=jnp.float32)
            weights, first_moment, second_moment = adam_update(weights, first_moment, second_moment, gradient, float(STEP_BASE + inner_step + 1))
        return weights
    params_new = lax.map(one_island, (tokens, targets, loss_mask, params, moment_one, moment_two))
    outer_mean = lax.optimization_barrier(jnp.sum(outer_delta, axis=0)) / outer_delta.shape[0]
    momentum_new = OUTER_MOMENTUM * outer_momentum + outer_mean
    outer_update = OUTER_RATE * (outer_mean + OUTER_MOMENTUM * momentum_new)
    return (params_new, momentum_new, outer_update)
```

```python
import jax
import jax.numpy as jnp
from jax import lax
from jax.sharding import PartitionSpec as P

ADAM_BETA_ONE = 0.9
ADAM_BETA_TWO = 0.95
ADAM_EPSILON = 1e-08
INNER_RATE = 0.005
WEIGHT_DECAY = 0.1
NORM_EPSILON = 1e-05
OUTER_RATE = 0.7
OUTER_MOMENTUM = 0.9
STEP_BASE = 1000


def adam_update(weights, first_moment, second_moment, gradient, count):
    first_moment = ADAM_BETA_ONE * first_moment + (1.0 - ADAM_BETA_ONE) * gradient
    second_moment = ADAM_BETA_TWO * second_moment + (1.0 - ADAM_BETA_TWO) * gradient * gradient
    first_hat = first_moment / (1.0 - ADAM_BETA_ONE**count)
    second_hat = second_moment / (1.0 - ADAM_BETA_TWO**count)
    weights = weights - INNER_RATE * (
        first_hat / (jnp.sqrt(second_hat) + ADAM_EPSILON) + WEIGHT_DECAY * weights
    )
    return (weights, first_moment, second_moment)


def per_device(
    tokens,
    targets,
    loss_mask,
    norm_gain,
    params,
    moment_one,
    moment_two,
    outer_delta,
    outer_momentum,
):
    fsdp_count = lax.axis_size("fsdp")
    token_island = tokens.shape[1] * fsdp_count
    weights = params[0]
    first_moment = moment_one[0]
    second_moment = moment_two[0]
    inputs_f = tokens[0].astype(jnp.float32)
    row_scale = lax.rsqrt(jnp.mean(inputs_f * inputs_f, axis=1) + NORM_EPSILON)
    scaled = (inputs_f * norm_gain).astype(jnp.bfloat16)
    keep_rows = loss_mask[0].astype(jnp.float32)
    goal_rows = targets[0].astype(jnp.float32)
    halves = []
    for h in range(2):
        cols = slice(128 * h, 128 * h + 128)
        halves.append([weights[:, cols], first_moment[:, cols], second_moment[:, cols], goal_rows[:, cols]])
    for inner_step in range(2):
        for h in range(2):
            weights, first_moment, second_moment, goal = halves[h]
            shard_rows = lax.all_gather(weights.astype(jnp.bfloat16), "fsdp", axis=0, tiled=True)
            projected = jnp.dot(scaled, shard_rows, preferred_element_type=jnp.float32)
            value_rows = row_scale[:, None] * projected
            residual_rows = (
                row_scale[:, None] * keep_rows[:, None] * (value_rows - goal) / token_island
            ).astype(jnp.bfloat16)
            gradient = lax.psum_scatter(
                lax.dot_general(
                    scaled, residual_rows, (((0,), (0,)), ((), ())), preferred_element_type=jnp.float32
                ).astype(jnp.bfloat16),
                "fsdp",
                scatter_dimension=0,
                tiled=True,
            ).astype(jnp.float32)
            halves[h][:3] = adam_update(
                weights, first_moment, second_moment, gradient, float(STEP_BASE + inner_step + 1)
            )
    weights = jnp.concatenate([halves[0][0], halves[1][0]], axis=1)
    island_count = lax.axis_size("island")
    planes = [[(y * 2 + h) * 4 + x for y in range(4) for x in range(4)] for h in range(2)]
    pieces = lax.all_to_all(
        outer_delta[0], "island", 0, 0, axis_index_groups=planes, tiled=True
    ).reshape(16, -1, outer_delta.shape[2])
    part = jnp.sum(pieces, axis=0)
    part = part + lax.ppermute(
        part, "island", [((y * 2 + h) * 4 + x, (y * 2 + 1 - h) * 4 + x) for y in range(4) for h in range(2) for x in range(4)]
    )
    summed = lax.all_gather(part, "island", axis_index_groups=planes, axis=0, tiled=True)
    outer_mean = summed / island_count
    momentum_new = OUTER_MOMENTUM * outer_momentum + outer_mean
    outer_update = OUTER_RATE * (outer_mean + OUTER_MOMENTUM * momentum_new)
    momentum_new, outer_update = (momentum_new, outer_update)
    return (weights[None], momentum_new, outer_update)


def solution(mesh):
    return jax.shard_map(
        per_device,
        mesh=mesh,
        in_specs=(
            P("island", "fsdp", None),
            P("island", "fsdp", None),
            P("island", "fsdp"),
            P(),
            P("island", "fsdp", None),
            P("island", "fsdp", None),
            P("island", "fsdp", None),
            P("island", "fsdp", None),
            P("fsdp", None),
        ),
        out_specs=(P("island", "fsdp", None), P("fsdp", None), P("fsdp", None)),
        check_vma=False,
    )
```

```python
import jax
import jax.numpy as jnp
from jax import lax
from jax.experimental import pallas as pl
from jax.experimental.pallas import tpu as pltpu
from jax.sharding import PartitionSpec as P

ADAM_BETA_ONE = 0.9
ADAM_BETA_TWO = 0.95
ADAM_EPSILON = 1e-08
INNER_RATE = 0.005
WEIGHT_DECAY = 0.1
NORM_EPSILON = 1e-05
OUTER_RATE = 0.7
OUTER_MOMENTUM = 0.9
STEP_BASE = 1000
CHIPS = 4
LANES = 128

RING = (
    [(2 * z, 2 * z + 2) for z in range(CHIPS - 1)]
    + [(2 * CHIPS - 2, 2 * CHIPS - 1)]
    + [(2 * z + 1, 2 * z - 1) for z in range(CHIPS - 1, 0, -1)]
    + [(1, 0)]
)
SWAP = [(i, i ^ 1) for i in range(2 * CHIPS)]


def after(array, *others):
    return lax.optimization_barrier((array, others))[0]


def conveyor(packet):
    return lax.ppermute(packet, "fsdp", RING)


def sibling(array):
    return lax.ppermute(array, "fsdp", SWAP)


def adam_update(weights, first_moment, second_moment, gradient, count):
    first_moment = ADAM_BETA_ONE * first_moment + (1.0 - ADAM_BETA_ONE) * gradient
    second_moment = ADAM_BETA_TWO * second_moment + (1.0 - ADAM_BETA_TWO) * gradient * gradient
    first_hat = first_moment / (1.0 - ADAM_BETA_ONE**count)
    second_hat = second_moment / (1.0 - ADAM_BETA_TWO**count)
    weights = weights - INNER_RATE * (
        first_hat / (jnp.sqrt(second_hat) + ADAM_EPSILON) + WEIGHT_DECAY * weights
    )
    return (weights, first_moment, second_moment)


def at_island(y, h, x):
    return (y * 2 + h) * 4 + x


HALVES = [(at_island(y, h, x), at_island(y, 1 - h, x)) for y in range(4) for h in range(2) for x in range(4)]


def turned(array, along_y, d):
    pairs = [
        (at_island(y, h, x), at_island((y + d) % 4, h, x) if along_y else at_island(y, h, (x + d) % 4))
        for y in range(4)
        for h in range(2)
        for x in range(4)
    ]
    return lax.ppermute(array, "island", pairs)


def outer_place(along_y):
    island = lax.axis_index("island")
    return island // 8 if along_y else island % 4


def outer_parts(array, along_y):
    place, rows = outer_place(along_y), array.shape[0] // 4
    quarter = lambda d: lax.dynamic_slice_in_dim(array, (place + d) % 4 * rows, rows, 0)
    total = quarter(0)
    for d in range(1, 4):
        total = total + turned(quarter(d), along_y, d)
    return total


def outer_whole(part, along_y):
    place, rows = outer_place(along_y), part.shape[0]
    whole = jnp.zeros((4 * rows, part.shape[1]), part.dtype)
    for d in range(4):
        came = turned(part, along_y, d) if d else part
        whole = lax.dynamic_update_slice_in_dim(whole, came, (place + 4 - d) % 4 * rows, 0)
    return whole


ROWS = 16


def scale_kernel(place_ref, tokens_ref, gain_ref, *refs):
    outs, scale_ref, held, total, came_in, went_out = refs[:-5], *refs[-5:]
    chip, upward = place_ref[0], place_ref[1] == 1
    width = held.shape[2]
    at, copies_in, copies_out = [], [], []
    for k in range(len(outs)):
        i, half = divmod(k, 2)
        at.append(jnp.where(upward, chip + (CHIPS - i), chip + i) % CHIPS * 2 + half)
        columns = pl.ds(pl.multiple_of(at[k] * width, LANES), width)
        copies_in.append(pltpu.make_async_copy(tokens_ref.at[:, columns], held.at[k], came_in.at[k]))
        copies_in[k].start()
        copies_out.append(pltpu.make_async_copy(held.at[k], outs[k], went_out.at[k]))
    total[...] = jnp.zeros_like(total)
    for k in range(len(outs)):
        copies_in[k].wait()

        @pl.loop(0, held.shape[1] // ROWS)
        def _(block):
            rows = pl.ds(pl.multiple_of(block * ROWS, ROWS), ROWS)
            part = total[rows, :]
            for lane in range(width // LANES):
                lanes = slice(lane * LANES, lane * LANES + LANES)
                values = held[k, rows, lanes].astype(jnp.float32)
                held[k, rows, lanes] = (values * gain_ref[at[k], :, lanes]).astype(jnp.bfloat16)
                part = part + values * values
            total[rows, :] = part

        copies_out[k].start()
    mean = jnp.sum(total[...], axis=1, keepdims=True) / (len(outs) * width)
    scale_ref[...] = lax.rsqrt(mean + NORM_EPSILON)
    for copy in copies_out:
        copy.wait()


def scale_tokens(tokens, gain, place, piece):
    rows, width = tokens.shape
    steps = width // piece
    anywhere = pl.BlockSpec(memory_space=pl.ANY)
    *scaled, scale = pl.pallas_call(
        scale_kernel,
        in_specs=[
            pl.BlockSpec(memory_space=pltpu.SMEM),
            anywhere,
            pl.BlockSpec(memory_space=pltpu.VMEM),
        ],
        out_specs=[anywhere] * steps + [pl.BlockSpec(memory_space=pltpu.VMEM)],
        out_shape=[jax.ShapeDtypeStruct((rows, piece), jnp.bfloat16)] * steps
        + [jax.ShapeDtypeStruct((rows, 1), jnp.float32)],
        scratch_shapes=[
            pltpu.VMEM((steps, rows, piece), jnp.bfloat16),
            pltpu.VMEM((rows, LANES), jnp.float32),
            pltpu.SemaphoreType.DMA((steps,)),
            pltpu.SemaphoreType.DMA((steps,)),
        ],
        compiler_params=pltpu.CompilerParams(vmem_limit_bytes=24 * 1024 * 1024),
        cost_estimate=pl.CostEstimate(flops=4 * rows * width, bytes_accessed=4 * rows * width, transcendentals=rows),
    )(place, tokens, gain.reshape(steps, 1, piece))
    return scaled, scale


def per_device(
    tokens,
    targets,
    loss_mask,
    norm_gain,
    params,
    moment_one,
    moment_two,
    outer_delta,
    outer_momentum,
):
    token_island = tokens.shape[1] * lax.axis_size("fsdp")
    me = lax.axis_index("fsdp")
    chip, core = me // 2, me % 2
    upward = core == 0
    place = jnp.where(upward, chip, CHIPS - 1 - chip)
    weights = params[0]
    piece = weights.shape[0]
    chunks = [slice(LANES * h, LANES * h + LANES) for h in range(weights.shape[1] // LANES)]

    def both(mine, other):
        return [jnp.where(upward, mine, other), jnp.where(upward, other, mine)]

    weights_bf = [weights[:, cols].astype(jnp.bfloat16) for cols in chunks]
    pieces = [both(w, sibling(w)) for w in weights_bf]
    states = [weights, moment_one[0], moment_two[0]]
    last = [None, None]

    def send(packet, half, *others):
        if last[half] is not None:
            others = (last[half],) + others
        last[half] = conveyor(after(packet, *others) if others else packet)
        return last[half]

    turn = jnp.stack([chip, upward.astype(jnp.int32)]).astype(jnp.int32)
    came_first = [pieces[0], [send(pieces[0][half], half) for half in range(2)]]
    scaled, scale_mine = scale_tokens(after(tokens[0], pieces[0]), norm_gain, turn, piece)
    came_first.append([send(came_first[1][half], half, scale_mine) for half in range(2)])
    scaled_other = [sibling(part) for part in scaled]
    row_data = jnp.concatenate([scale_mine, loss_mask[0].astype(jnp.float32)[:, None]], axis=1)
    row_data = jnp.concatenate([row_data, sibling(row_data)], axis=0)
    row_scale, keep_rows = row_data[:, :1], row_data[:, 1:]
    goal = after(targets[0], came_first[1])
    goal_rows = jnp.concatenate([goal, sibling(goal)], axis=0).astype(jnp.float32)
    near = [
        [
            jnp.concatenate([scaled[2 * i + half], scaled_other[(CHIPS - i) % CHIPS * 2 + half]], axis=0)
            for half in range(2)
        ]
        for i in range(CHIPS)
    ]
    own_columns = jnp.where(upward, near[0][0], near[0][1])
    outer = outer_parts(after(outer_delta[0], came_first[1]), 1)
    came_first.append([send(came_first[2][half], half) for half in range(2)])
    states_other = [sibling(after(v, came_first[3])) for v in states]
    pair_states = [
        [lax.optimization_barrier(both(v[:, cols], o[:, cols])) for v, o in zip(states, states_other)]
        for cols in chunks
    ]

    def project(cols, own_piece, came):
        total = jnp.dot(own_columns, own_piece, preferred_element_type=jnp.float32)
        for i in range(1, CHIPS):
            for half in range(2):
                term = jnp.dot(near[i][half], came[i][half], preferred_element_type=jnp.float32)
                total = total + jnp.where(place >= i, term, 0.0)
        other = sibling(total)
        rows = total.shape[0] // 2
        total = total + jnp.concatenate([other[rows:], other[:rows]], axis=0)
        value_rows = row_scale * total
        return (
            row_scale * keep_rows * (value_rows - goal_rows[:, cols]) / token_island
        ).astype(jnp.bfloat16)

    def gradient_of(columns, residual):
        return lax.dot_general(columns, residual, (((0,), (0,)), ((), ())), preferred_element_type=jnp.float32)

    def sum_packet(i, half, residual, came):
        term = gradient_of(near[i][half], residual)
        if came is not None:
            term = term + jnp.where(place >= 1, came[half].astype(jnp.float32), 0.0)
        return term.astype(jnp.bfloat16)

    def slot(gather, summing, *others):
        out = []
        for half in range(2):
            packet = None
            if gather is not None:
                packet = gather[half]
            if summing is not None:
                r, residual, came = summing
                term = sum_packet(r, half, residual, came)
                packet = term if packet is None else jnp.where(place >= r, packet, term)
            out.append(send(packet, half, *others))
        return out

    def own_of(pair):
        return jnp.where(upward, pair[0], pair[1])

    first_grad = [None, None]
    second_pieces = [None, None]

    def received(mine, other):
        below = jnp.where(place >= 1, mine.astype(jnp.float32), 0.0)
        return below + jnp.where(place <= CHIPS - 2, other.astype(jnp.float32), 0.0)

    def first_step(h, own, came):
        grads, fresh = [], []
        for half in range(2):
            grad = received(came[half], sibling(came[half])) + gradient_of(near[0][half], own)
            state = [v[half] for v in pair_states[h]]
            fresh.append(adam_update(*state, grad, float(STEP_BASE + 1))[0].astype(jnp.bfloat16))
            grads.append(grad)
        first_grad[h] = own_of(grads)
        second_pieces[h] = fresh

    def last_step(h, own, came):
        grad = received(own_of(came), sibling(jnp.where(upward, came[1], came[0]))) + gradient_of(own_columns, own)
        state = adam_update(*[v[:, chunks[h]] for v in states], first_grad[h], float(STEP_BASE + 1))
        return adam_update(*state, grad, float(STEP_BASE + 2))[0]

    a, b = 0, 1
    residual_a = project(chunks[a], weights_bf[a], came_first)
    def overlap(gather_pieces, residual, *others):
        came = [gather_pieces, slot(gather_pieces, None, *others)]
        for r in range(1, CHIPS - 1):
            came.append(slot(came[-1], (r, residual, came[-1] if r > 1 else None)))
        return came, slot(None, (CHIPS - 1, residual, came[-1]))

    came_b, sums_a = overlap(pieces[b], residual_a, outer)
    outer = outer_parts(outer, 0)
    first_step(a, residual_a, sums_a)
    residual_b = project(chunks[b], weights_bf[b], came_b)

    came_a, sums_b = overlap(second_pieces[a], residual_b, outer)
    outer = outer + lax.ppermute(after(outer, came_a[1]), "island", HALVES)
    first_step(b, residual_b, sums_b)
    residual_a = project(chunks[a], own_of(second_pieces[a]), came_a)

    outer = outer_whole(outer, 0)
    came_b, sums_a = overlap(second_pieces[b], residual_a, outer)
    outer = outer_whole(after(outer, came_b[1]), 1)
    weights_a = last_step(a, residual_a, sums_a)
    residual_b = project(chunks[b], own_of(second_pieces[b]), came_b)

    outer_mean = outer / lax.axis_size("island")
    momentum_new = OUTER_MOMENTUM * outer_momentum + outer_mean
    outer_update = OUTER_RATE * (outer_mean + OUTER_MOMENTUM * momentum_new)

    came = None
    for r in range(1, CHIPS):
        came = slot(None, (r, residual_b, came), *([weights_a, momentum_new, outer_update] if r == CHIPS - 1 else []))
    weights = jnp.concatenate([weights_a, last_step(b, residual_b, came)], axis=1)

    return (weights[None], momentum_new, outer_update)


def solution(mesh):
    return jax.shard_map(
        per_device,
        mesh=mesh,
        in_specs=(
            P("island", "fsdp", None),
            P("island", "fsdp", None),
            P("island", "fsdp"),
            P(),
            P("island", "fsdp", None),
            P("island", "fsdp", None),
            P("island", "fsdp", None),
            P("island", "fsdp", None),
            P("fsdp", None),
        ),
        out_specs=(P("island", "fsdp", None), P("fsdp", None), P("fsdp", None)),
        check_vma=False,
    )
```

```python
import jax
import jax.numpy as jnp
from jax import lax
from jax.experimental import pallas as pl
from jax.experimental.pallas import tpu as pltpu
from jax.sharding import PartitionSpec as P

ADAM_BETA_ONE = 0.9
ADAM_BETA_TWO = 0.95
ADAM_EPSILON = 1e-08
INNER_RATE = 0.005
WEIGHT_DECAY = 0.1
NORM_EPSILON = 1e-05
OUTER_RATE = 0.7
OUTER_MOMENTUM = 0.9
STEP_BASE = 1000
CHIPS = 4
LANES = 128

RING = (
    [(2 * z, 2 * z + 2) for z in range(CHIPS - 1)]
    + [(2 * CHIPS - 2, 2 * CHIPS - 1)]
    + [(2 * z + 1, 2 * z - 1) for z in range(CHIPS - 1, 0, -1)]
    + [(1, 0)]
)
SWAP = [(i, i ^ 1) for i in range(2 * CHIPS)]


def after(array, *others):
    return lax.optimization_barrier((array, others))[0]


def conveyor(packet):
    return lax.ppermute(packet, "fsdp", RING)


def sibling(array):
    return lax.ppermute(array, "fsdp", SWAP)


def adam_update(weights, first_moment, second_moment, gradient, count):
    first_moment = ADAM_BETA_ONE * first_moment + (1.0 - ADAM_BETA_ONE) * gradient
    second_moment = ADAM_BETA_TWO * second_moment + (1.0 - ADAM_BETA_TWO) * gradient * gradient
    first_hat = first_moment / (1.0 - ADAM_BETA_ONE**count)
    second_hat = second_moment / (1.0 - ADAM_BETA_TWO**count)
    weights = weights - INNER_RATE * (
        first_hat / (jnp.sqrt(second_hat) + ADAM_EPSILON) + WEIGHT_DECAY * weights
    )
    return (weights, first_moment, second_moment)


def at_island(y, h, x):
    return (y * 2 + h) * 4 + x


def across(array, y=0, h=0, x=0):
    pairs = [
        (at_island(p, q, r), at_island(p ^ y, q ^ h, r ^ x)) for p in range(4) for q in range(2) for r in range(4)
    ]
    return lax.ppermute(array, "island", pairs)


def outer_bit(y=0, x=0):
    island = lax.axis_index("island")
    return (island // 8) & y != 0 if y else (island % 4) & x != 0


def outer_fold(array, **bits):
    rows, upper = array.shape[0] // 2, outer_bit(**bits)
    keep = jnp.where(upper, array[rows:], array[:rows])
    return keep + across(jnp.where(upper, array[:rows], array[rows:]), **bits)


def outer_join(array, **bits):
    other, upper = across(array, **bits), outer_bit(**bits)
    return jnp.concatenate([jnp.where(upper, other, array), jnp.where(upper, array, other)], axis=0)


OUTER_STEPS = [
    lambda v: outer_fold(v, x=1),
    lambda v: outer_fold(v, x=2),
    lambda v: outer_fold(v, y=1),
    lambda v: outer_fold(v, y=2),
    lambda v: v + across(v, h=1),
    lambda v: outer_join(v, y=2),
    lambda v: outer_join(v, y=1),
    lambda v: outer_join(v, x=2),
    lambda v: outer_join(v, x=1),
]
OUTER_WHEN = [(1, 2), (2, 3), (3, 4), (4, 5), (5, 7), (10, 11), (13, 14), (14, 15), (15, 17)]


ROWS = 16
NO_COST = pl.CostEstimate(flops=0, bytes_accessed=0, transcendentals=0)


def lay_kernel(*refs):
    count = (len(refs) - 1) // 3
    tops, bottoms, outs, done = refs[:count], refs[count : 2 * count], refs[2 * count : 3 * count], refs[-1]
    copies = []
    for k in range(count):
        rows = tops[k].shape[0]
        copies.append(pltpu.make_async_copy(tops[k], outs[k].at[pl.ds(0, rows), :], done.at[2 * k]))
        copies.append(pltpu.make_async_copy(bottoms[k], outs[k].at[pl.ds(rows, rows), :], done.at[2 * k + 1]))
    for copy in copies:
        copy.start()
    for copy in copies:
        copy.wait()


def lay(tops, bottoms):
    rows, width = tops[0].shape
    count = len(tops)
    anywhere = pl.BlockSpec(memory_space=pl.ANY)
    return pl.pallas_call(
        lay_kernel,
        in_specs=[anywhere] * (2 * count),
        out_specs=[anywhere] * count,
        out_shape=[jax.ShapeDtypeStruct((2 * rows, width), tops[0].dtype)] * count,
        scratch_shapes=[pltpu.SemaphoreType.DMA((2 * count,))],
        compiler_params=pltpu.CompilerParams(vmem_limit_bytes=1024 * 1024),
        cost_estimate=NO_COST,
    )(*tops, *bottoms)


def scale_kernel(place_ref, tokens_ref, gain_ref, *refs):
    outs, scale_ref, held, total, came_in, went_out = refs[:-5], *refs[-5:]
    chip, upward = place_ref[0], place_ref[1] == 1
    width = held.shape[2]
    at, copies_in, copies_out = [], [], []
    for k in range(len(outs)):
        i, half = divmod(k, 2)
        at.append(jnp.where(upward, chip + (CHIPS - i), chip + i) % CHIPS * 2 + half)
        columns = pl.ds(pl.multiple_of(at[k] * width, LANES), width)
        copies_in.append(pltpu.make_async_copy(tokens_ref.at[:, columns], held.at[k], came_in.at[k]))
        copies_in[k].start()
        copies_out.append(pltpu.make_async_copy(held.at[k], outs[k], went_out.at[k]))
    total[...] = jnp.zeros_like(total)
    for k in range(len(outs)):
        copies_in[k].wait()

        @pl.loop(0, held.shape[1] // ROWS)
        def _(block):
            rows = pl.ds(pl.multiple_of(block * ROWS, ROWS), ROWS)
            part = total[rows, :]
            for lane in range(width // LANES):
                lanes = slice(lane * LANES, lane * LANES + LANES)
                values = held[k, rows, lanes].astype(jnp.float32)
                held[k, rows, lanes] = (values * gain_ref[at[k], :, lanes]).astype(jnp.bfloat16)
                part = part + values * values
            total[rows, :] = part

        copies_out[k].start()
    mean = jnp.sum(total[...], axis=1, keepdims=True) / (len(outs) * width)
    scale_ref[...] = lax.rsqrt(mean + NORM_EPSILON)
    for copy in copies_out:
        copy.wait()


def scale_tokens(tokens, gain, place, piece):
    rows, width = tokens.shape
    steps = width // piece
    anywhere = pl.BlockSpec(memory_space=pl.ANY)
    *scaled, scale = pl.pallas_call(
        scale_kernel,
        in_specs=[
            pl.BlockSpec(memory_space=pltpu.SMEM),
            pl.BlockSpec(memory_space=pltpu.HBM),
            pl.BlockSpec(memory_space=pltpu.VMEM),
        ],
        out_specs=[anywhere] * steps + [pl.BlockSpec(memory_space=pltpu.VMEM)],
        out_shape=[jax.ShapeDtypeStruct((rows, piece), jnp.bfloat16)] * steps
        + [jax.ShapeDtypeStruct((rows, 1), jnp.float32)],
        scratch_shapes=[
            pltpu.VMEM((steps, rows, piece), jnp.bfloat16),
            pltpu.VMEM((rows, LANES), jnp.float32),
            pltpu.SemaphoreType.DMA((steps,)),
            pltpu.SemaphoreType.DMA((steps,)),
        ],
        compiler_params=pltpu.CompilerParams(vmem_limit_bytes=10 * 1024 * 1024),
        cost_estimate=NO_COST,
    )(place, tokens, gain.reshape(steps, 1, piece))
    return scaled, scale


def per_device(
    tokens,
    targets,
    loss_mask,
    norm_gain,
    params,
    moment_one,
    moment_two,
    outer_delta,
    outer_momentum,
):
    token_island = tokens.shape[1] * lax.axis_size("fsdp")
    me = lax.axis_index("fsdp")
    chip, core = me // 2, me % 2
    upward = core == 0
    place = jnp.where(upward, chip, CHIPS - 1 - chip)
    weights = params[0]
    piece = weights.shape[0]
    chunks = [slice(LANES * h, LANES * h + LANES) for h in range(weights.shape[1] // LANES)]

    def both(mine, other):
        return [jnp.where(upward, mine, other), jnp.where(upward, other, mine)]

    weights_bf = [weights[:, chunks[0]].astype(jnp.bfloat16)]
    pieces = [both(weights_bf[0], sibling(weights_bf[0]))]
    states = [weights, moment_one[0], moment_two[0]]
    last = [None, None]

    slots = [0, 0]
    outer = [outer_delta[0]]

    def send(packet, half, *others):
        slots[half] += 1
        steps = list(zip(OUTER_STEPS, OUTER_WHEN))
        if half == 0 and any(need == slots[0] for _, (_, need) in steps):
            others += (outer[0],)
        if last[half] is not None:
            others = (last[half],) + others
        if half == 0 and 2 <= slots[0] <= 4:
            others += (last[1],)
        packet = after(packet, *others) if others else packet
        for step, (start, _) in steps:
            if half == 1 and start == slots[1]:
                outer[0] = step(after(outer[0], packet) if start > 1 else outer[0])
        last[half] = conveyor(packet)
        return last[half]

    turn = jnp.stack([chip, upward.astype(jnp.int32)]).astype(jnp.int32)
    came_first = [pieces[0], [send(pieces[0][half], half) for half in range(2)]]
    scaled, scale_mine = scale_tokens(tokens[0], norm_gain, after(turn, pieces[0]), piece)
    came_first.append([send(came_first[1][half], half, scale_mine) for half in range(2)])
    scaled_other = [sibling(part) for part in scaled]
    near = [None] * CHIPS
    for group in ((1, 2), (3, 0)):
        wanted = [(i, half) for i in group for half in range(2)]
        laid = lay(
            [scaled[2 * i + half] for i, half in wanted],
            [scaled_other[(CHIPS - i) % CHIPS * 2 + half] for i, half in wanted],
        )
        for n, i in enumerate(group):
            near[i] = list(laid[2 * n : 2 * n + 2])
    waits = [near[1] + near[2], []]
    came_first.append([send(came_first[2][half], half, *waits[half]) for half in range(2)])
    weights_bf.append(after(weights, came_first[2][1])[:, chunks[1]].astype(jnp.bfloat16))
    pieces.append(both(weights_bf[1], sibling(weights_bf[1])))
    row_data = jnp.concatenate([scale_mine, loss_mask[0].astype(jnp.float32)[:, None]], axis=1)
    row_data = after(row_data, came_first[2][1])
    row_data = jnp.concatenate([row_data, sibling(row_data)], axis=0)
    row_scale, keep_rows = row_data[:, :1], row_data[:, 1:]
    goal = after(targets[0], came_first[2][1])
    goal_rows = jnp.concatenate([goal, sibling(goal)], axis=0).astype(jnp.float32)
    own_columns = jnp.where(upward, near[0][0], near[0][1])
    states_other = [sibling(after(v, came_first[3])) for v in states]
    pair_states = [
        [lax.optimization_barrier(both(v[:, cols], o[:, cols])) for v, o in zip(states, states_other)]
        for cols in chunks
    ]

    def project(cols, own_piece, came, *others):
        total = jnp.dot(own_columns, own_piece, preferred_element_type=jnp.float32)
        for i in range(1, CHIPS):
            for half in range(2):
                use = came[i][half]
                if (i, half) != (CHIPS - 1, 1):
                    use = after(use, came[i + half][1 - half])
                term = jnp.dot(near[i][half], use, preferred_element_type=jnp.float32)
                total = total + jnp.where(place >= i, term, 0.0)
        other = sibling(total)
        rows = total.shape[0] // 2
        total = total + jnp.concatenate([other[rows:], other[:rows]], axis=0)
        value_rows = row_scale * (after(total, *others) if others else total)
        return (
            row_scale * keep_rows * (value_rows - goal_rows[:, cols]) / token_island
        ).astype(jnp.bfloat16)

    def gradient_of(columns, residual):
        return lax.dot_general(columns, residual, (((0,), (0,)), ((), ())), preferred_element_type=jnp.float32)

    def sum_packet(i, half, residual, came):
        term = gradient_of(near[i][half], residual)
        if came is not None:
            term = term + jnp.where(place >= 1, came[half].astype(jnp.float32), 0.0)
        return term.astype(jnp.bfloat16)

    def slot(gather, summing, *others):
        out = []
        for half in range(2):
            packet = None
            if gather is not None:
                packet = gather[half]
            if summing is not None:
                r, residual, came = summing
                term = sum_packet(r, half, residual, came)
                packet = term if packet is None else jnp.where(place >= r, packet, term)
            out.append(send(packet, half, *others))
        return out

    def own_of(pair):
        return jnp.where(upward, pair[0], pair[1])

    first_grad = [None, None]
    second_pieces = [None, None]

    def received(mine, other):
        below = jnp.where(place >= 1, mine.astype(jnp.float32), 0.0)
        return below + jnp.where(place <= CHIPS - 2, other.astype(jnp.float32), 0.0)

    def first_step(h, own, came):
        grads, fresh = [], []
        for half in range(2):
            mine = after(came[half], fresh[0]) if half else came[half]
            grad = received(mine, sibling(mine)) + gradient_of(near[0][half], own)
            state = [v[half] for v in pair_states[h]]
            fresh.append(adam_update(*state, grad, float(STEP_BASE + 1))[0].astype(jnp.bfloat16))
            grads.append(grad)
        first_grad[h] = own_of(grads)
        second_pieces[h] = fresh

    def last_step(h, own, came):
        grad = received(own_of(came), sibling(jnp.where(upward, came[1], came[0]))) + gradient_of(own_columns, own)
        state = adam_update(*[v[:, chunks[h]] for v in states], first_grad[h], float(STEP_BASE + 1))
        return adam_update(*state, grad, float(STEP_BASE + 2))[0]

    a, b = 0, 1
    waits = [near[0] + near[3], []]
    first_b = [send(pieces[b][half], half, *waits[half]) for half in range(2)]
    residual_a = project(chunks[a], weights_bf[a], came_first, first_b[1])
    def overlap(gather_pieces, first, residual, *others):
        came = [gather_pieces, first]
        for r in range(1, CHIPS - 1):
            came.append(slot(came[-1], (r, residual, came[-1] if r > 1 else None), *(others if r == 1 else [])))
        return came, slot(None, (CHIPS - 1, residual, came[-1]))

    came_b, sums_a = overlap(pieces[b], first_b, residual_a, pair_states)
    first_step(a, residual_a, sums_a)
    residual_b = project(chunks[b], weights_bf[b], came_b)

    came_a, sums_b = overlap(second_pieces[a], slot(second_pieces[a], None), residual_b)
    first_step(b, residual_b, sums_b)
    residual_a = project(chunks[a], own_of(second_pieces[a]), came_a)

    came_b, sums_a = overlap(second_pieces[b], slot(second_pieces[b], None), residual_a)
    weights_a = last_step(a, residual_a, sums_a)
    residual_b = project(chunks[b], own_of(second_pieces[b]), came_b)

    came = slot(None, (1, residual_b, None))
    came = slot(None, (2, residual_b, came))
    weights = jnp.concatenate([weights_a, weights[:, chunks[b]]], axis=1)
    came = slot(None, (3, residual_b, came), weights)
    weights = lax.dynamic_update_slice(weights, last_step(b, residual_b, came), (0, chunks[b].start))
    outer_mean = outer[0] / lax.axis_size("island")
    momentum_new = OUTER_MOMENTUM * outer_momentum + outer_mean
    outer_update = OUTER_RATE * (outer_mean + OUTER_MOMENTUM * momentum_new)
    return (weights[None], momentum_new, outer_update)


def solution(mesh):
    return jax.shard_map(
        per_device,
        mesh=mesh,
        in_specs=(
            P("island", "fsdp", None),
            P("island", "fsdp", None),
            P("island", "fsdp"),
            P(),
            P("island", "fsdp", None),
            P("island", "fsdp", None),
            P("island", "fsdp", None),
            P("island", "fsdp", None),
            P("fsdp", None),
        ),
        out_specs=(P("island", "fsdp", None), P("fsdp", None), P("fsdp", None)),
        check_vma=False,
    )
```

```python
import jax
import jax.numpy as jnp
from jax import lax
from jax.experimental import pallas as pl
from jax.experimental.pallas import tpu as pltpu
from jax.sharding import PartitionSpec as P

ADAM_BETA_ONE = 0.9
ADAM_BETA_TWO = 0.95
ADAM_EPSILON = 1e-08
INNER_RATE = 0.005
WEIGHT_DECAY = 0.1
NORM_EPSILON = 1e-05
OUTER_RATE = 0.7
OUTER_MOMENTUM = 0.9
STEP_BASE = 1000
CHIPS = 4
LANES = 128

RING = (
    [(2 * z, 2 * z + 2) for z in range(CHIPS - 1)]
    + [(2 * CHIPS - 2, 2 * CHIPS - 1)]
    + [(2 * z + 1, 2 * z - 1) for z in range(CHIPS - 1, 0, -1)]
    + [(1, 0)]
)
SWAP = [(i, i ^ 1) for i in range(2 * CHIPS)]


def after(array, *others):
    return lax.optimization_barrier((array, others))[0]


def conveyor(packet):
    return lax.ppermute(packet, "fsdp", RING)


def sibling(array):
    return lax.ppermute(array, "fsdp", SWAP)


def adam_update(weights, first_moment, second_moment, gradient, count):
    first_moment = ADAM_BETA_ONE * first_moment + (1.0 - ADAM_BETA_ONE) * gradient
    second_moment = ADAM_BETA_TWO * second_moment + (1.0 - ADAM_BETA_TWO) * gradient * gradient
    first_hat = first_moment / (1.0 - ADAM_BETA_ONE**count)
    second_hat = second_moment / (1.0 - ADAM_BETA_TWO**count)
    weights = weights - INNER_RATE * (
        first_hat / (jnp.sqrt(second_hat) + ADAM_EPSILON) + WEIGHT_DECAY * weights
    )
    return (weights, first_moment, second_moment)


def at_island(y, h, x):
    return (y * 2 + h) * 4 + x


def across(array, y=0, h=0, x=0):
    pairs = [
        (at_island(p, q, r), at_island(p ^ y, q ^ h, r ^ x)) for p in range(4) for q in range(2) for r in range(4)
    ]
    return lax.ppermute(array, "island", pairs)


def outer_bit(y=0, x=0):
    island = lax.axis_index("island")
    return (island // 8) & y != 0 if y else (island % 4) & x != 0


def outer_fold(array, **bits):
    rows, upper = array.shape[0] // 2, outer_bit(**bits)
    keep = jnp.where(upper, array[rows:], array[:rows])
    return keep + across(jnp.where(upper, array[:rows], array[rows:]), **bits)


def outer_join(array, **bits):
    other, upper = across(array, **bits), outer_bit(**bits)
    return jnp.concatenate([jnp.where(upper, other, array), jnp.where(upper, array, other)], axis=0)


OUTER_STEPS = [
    lambda v: outer_fold(v, x=1),
    lambda v: outer_fold(v, x=2),
    lambda v: outer_fold(v, y=1),
    lambda v: outer_fold(v, y=2),
    lambda v: v + across(v, h=1),
    lambda v: outer_join(v, y=2),
    lambda v: outer_join(v, y=1),
    lambda v: outer_join(v, x=2),
    lambda v: outer_join(v, x=1),
]
OUTER_WHEN = [(1, 2), (2, 3), (3, 4), (4, 5), (7, 10), (10, 11), (13, 14), (14, 15), (15, 17)]


ROWS = 16
NO_COST = pl.CostEstimate(flops=0, bytes_accessed=0, transcendentals=0)


def lay_kernel(*refs):
    count = (len(refs) - 1) // 3
    tops, bottoms, outs, done = refs[:count], refs[count : 2 * count], refs[2 * count : 3 * count], refs[-1]
    copies = []
    for k in range(count):
        rows = tops[k].shape[0]
        copies.append(pltpu.make_async_copy(tops[k], outs[k].at[pl.ds(0, rows), :], done.at[2 * k]))
        copies.append(pltpu.make_async_copy(bottoms[k], outs[k].at[pl.ds(rows, rows), :], done.at[2 * k + 1]))
    for copy in copies:
        copy.start()
    for copy in copies:
        copy.wait()


def lay(tops, bottoms):
    rows, width = tops[0].shape
    count = len(tops)
    anywhere = pl.BlockSpec(memory_space=pl.ANY)
    return pl.pallas_call(
        lay_kernel,
        in_specs=[anywhere] * (2 * count),
        out_specs=[anywhere] * count,
        out_shape=[jax.ShapeDtypeStruct((2 * rows, width), tops[0].dtype)] * count,
        scratch_shapes=[pltpu.SemaphoreType.DMA((2 * count,))],
        compiler_params=pltpu.CompilerParams(vmem_limit_bytes=1024 * 1024),
        cost_estimate=NO_COST,
    )(*tops, *bottoms)


def scale_kernel(place_ref, tokens_ref, gain_ref, *refs):
    outs, scale_ref, held, total, came_in, went_out = refs[:-5], *refs[-5:]
    chip, upward = place_ref[0], place_ref[1] == 1
    width = held.shape[2]
    at, copies_in, copies_out = [], [], []
    for k in range(len(outs)):
        i, half = divmod(k, 2)
        at.append(jnp.where(upward, chip + (CHIPS - i), chip + i) % CHIPS * 2 + half)
        columns = pl.ds(pl.multiple_of(at[k] * width, LANES), width)
        copies_in.append(pltpu.make_async_copy(tokens_ref.at[:, columns], held.at[k], came_in.at[k]))
        copies_in[k].start()
        copies_out.append(pltpu.make_async_copy(held.at[k], outs[k], went_out.at[k]))
    total[...] = jnp.zeros_like(total)
    for k in range(len(outs)):
        copies_in[k].wait()

        @pl.loop(0, held.shape[1] // ROWS)
        def _(block):
            rows = pl.ds(pl.multiple_of(block * ROWS, ROWS), ROWS)
            part = total[rows, :]
            for lane in range(width // LANES):
                lanes = slice(lane * LANES, lane * LANES + LANES)
                values = held[k, rows, lanes].astype(jnp.float32)
                held[k, rows, lanes] = (values * gain_ref[at[k], :, lanes]).astype(jnp.bfloat16)
                part = part + values * values
            total[rows, :] = part

        copies_out[k].start()
    mean = jnp.sum(total[...], axis=1, keepdims=True) / (len(outs) * width)
    scale_ref[...] = lax.rsqrt(mean + NORM_EPSILON)
    for copy in copies_out:
        copy.wait()


def scale_tokens(tokens, gain, place, piece):
    rows, width = tokens.shape
    steps = width // piece
    anywhere = pl.BlockSpec(memory_space=pl.ANY)
    *scaled, scale = pl.pallas_call(
        scale_kernel,
        in_specs=[
            pl.BlockSpec(memory_space=pltpu.SMEM),
            pl.BlockSpec(memory_space=pltpu.HBM),
            pl.BlockSpec(memory_space=pltpu.VMEM),
        ],
        out_specs=[anywhere] * steps + [pl.BlockSpec(memory_space=pltpu.VMEM)],
        out_shape=[jax.ShapeDtypeStruct((rows, piece), jnp.bfloat16)] * steps
        + [jax.ShapeDtypeStruct((rows, 1), jnp.float32)],
        scratch_shapes=[
            pltpu.VMEM((steps, rows, piece), jnp.bfloat16),
            pltpu.VMEM((rows, LANES), jnp.float32),
            pltpu.SemaphoreType.DMA((steps,)),
            pltpu.SemaphoreType.DMA((steps,)),
        ],
        compiler_params=pltpu.CompilerParams(vmem_limit_bytes=10 * 1024 * 1024),
        cost_estimate=NO_COST,
    )(place, tokens, gain.reshape(steps, 1, piece))
    return scaled, scale


def per_device(
    tokens,
    targets,
    loss_mask,
    norm_gain,
    params,
    moment_one,
    moment_two,
    outer_delta,
    outer_momentum,
):
    token_island = tokens.shape[1] * lax.axis_size("fsdp")
    me = lax.axis_index("fsdp")
    chip, core = me // 2, me % 2
    upward = core == 0
    place = jnp.where(upward, chip, CHIPS - 1 - chip)
    weights = params[0]
    piece = weights.shape[0]
    chunks = [slice(LANES * h, LANES * h + LANES) for h in range(weights.shape[1] // LANES)]

    def both(mine, other):
        return [jnp.where(upward, mine, other), jnp.where(upward, other, mine)]

    weights_bf = [weights[:, chunks[0]].astype(jnp.bfloat16)]
    pieces = [both(weights_bf[0], sibling(weights_bf[0]))]
    states = [weights, moment_one[0], moment_two[0]]
    last = [None, None]

    slots = [0, 0]
    outer = [outer_delta[0]]

    def send(packet, half, *others):
        slots[half] += 1
        steps = list(zip(OUTER_STEPS, OUTER_WHEN))
        if half == 0 and any(need == slots[0] for _, (_, need) in steps):
            others += (outer[0],)
        if last[half] is not None:
            others = (last[half],) + others
        if half == 0 and 2 <= slots[0] <= 4:
            others += (last[1],)
        packet = after(packet, *others) if others else packet
        for step, (start, _) in steps:
            if half == 1 and start == slots[1]:
                outer[0] = step(after(outer[0], packet) if start > 1 else outer[0])
        last[half] = conveyor(packet)
        return last[half]

    turn = jnp.stack([chip, upward.astype(jnp.int32)]).astype(jnp.int32)
    came_first = [pieces[0], [send(pieces[0][half], half) for half in range(2)]]
    scaled, scale_mine = scale_tokens(tokens[0], norm_gain, after(turn, pieces[0]), piece)
    came_first.append([send(came_first[1][half], half, scale_mine) for half in range(2)])
    scaled_other = [sibling(part) for part in scaled]
    near = [None] * CHIPS
    for group in ((1, 2), (3, 0)):
        wanted = [(i, half) for i in group for half in range(2)]
        laid = lay(
            [scaled[2 * i + half] for i, half in wanted],
            [scaled_other[(CHIPS - i) % CHIPS * 2 + half] for i, half in wanted],
        )
        for n, i in enumerate(group):
            near[i] = list(laid[2 * n : 2 * n + 2])
    waits = [near[1] + near[2], []]
    came_first.append([send(came_first[2][half], half, *waits[half]) for half in range(2)])
    weights_bf.append(after(weights, came_first[2][1])[:, chunks[1]].astype(jnp.bfloat16))
    pieces.append(both(weights_bf[1], sibling(weights_bf[1])))
    row_data = jnp.concatenate([scale_mine, loss_mask[0].astype(jnp.float32)[:, None]], axis=1)
    row_data = after(row_data, came_first[2][1])
    row_data = jnp.concatenate([row_data, sibling(row_data)], axis=0)
    row_scale, keep_rows = row_data[:, :1], row_data[:, 1:]
    goal = after(targets[0], came_first[2][1])
    goal_rows = jnp.concatenate([goal, sibling(goal)], axis=0).astype(jnp.float32)
    own_columns = jnp.where(upward, near[0][0], near[0][1])
    states_other = [sibling(after(v, came_first[3])) for v in states]
    pair_states = [
        [lax.optimization_barrier(both(v[:, cols], o[:, cols])) for v, o in zip(states, states_other)]
        for cols in chunks
    ]

    def project(cols, own_piece, came, *others):
        total = jnp.dot(own_columns, own_piece, preferred_element_type=jnp.float32)
        for i in range(1, CHIPS):
            for half in range(2):
                use = came[i][half]
                if (i, half) != (CHIPS - 1, 1):
                    use = after(use, came[i + half][1 - half])
                term = jnp.dot(near[i][half], use, preferred_element_type=jnp.float32)
                total = total + jnp.where(place >= i, term, 0.0)
        other = sibling(total)
        rows = total.shape[0] // 2
        total = total + jnp.concatenate([other[rows:], other[:rows]], axis=0)
        value_rows = row_scale * (after(total, *others) if others else total)
        return (
            row_scale * keep_rows * (value_rows - goal_rows[:, cols]) / token_island
        ).astype(jnp.bfloat16)

    def gradient_of(columns, residual):
        return lax.dot_general(columns, residual, (((0,), (0,)), ((), ())), preferred_element_type=jnp.float32)

    def sum_packet(i, half, residual, came):
        term = gradient_of(near[i][half], residual)
        if came is not None:
            term = term + jnp.where(place >= 1, came[half].astype(jnp.float32), 0.0)
        return term.astype(jnp.bfloat16)

    def slot(gather, summing, *others):
        out = []
        for half in range(2):
            packet = None
            if gather is not None:
                packet = gather[half]
            if summing is not None:
                r, residual, came = summing
                term = sum_packet(r, half, residual, came)
                packet = term if packet is None else jnp.where(place >= r, packet, term)
            out.append(send(packet, half, *others))
        return out

    def own_of(pair):
        return jnp.where(upward, pair[0], pair[1])

    first_grad = [None, None]
    second_pieces = [None, None]

    def received(mine, other):
        below = jnp.where(place >= 1, mine.astype(jnp.float32), 0.0)
        return below + jnp.where(place <= CHIPS - 2, other.astype(jnp.float32), 0.0)

    def first_step(h, own, came):
        grads, fresh = [], []
        for half in range(2):
            mine = after(came[half], fresh[0]) if half else came[half]
            grad = received(mine, sibling(mine)) + gradient_of(near[0][half], own)
            state = [v[half] for v in pair_states[h]]
            fresh.append(adam_update(*state, grad, float(STEP_BASE + 1))[0].astype(jnp.bfloat16))
            grads.append(grad)
        first_grad[h] = own_of(grads)
        second_pieces[h] = fresh

    def last_step(h, own, came):
        grad = received(own_of(came), sibling(jnp.where(upward, came[1], came[0]))) + gradient_of(own_columns, own)
        state = adam_update(*[v[:, chunks[h]] for v in states], first_grad[h], float(STEP_BASE + 1))
        return adam_update(*state, grad, float(STEP_BASE + 2))[0]

    a, b = 0, 1
    waits = [near[0] + near[3], []]
    first_b = [send(pieces[b][half], half, *waits[half]) for half in range(2)]
    residual_a = project(chunks[a], weights_bf[a], came_first, first_b[1])
    def overlap(gather_pieces, first, residual, *others):
        came = [gather_pieces, first]
        for r in range(1, CHIPS - 1):
            came.append(slot(came[-1], (r, residual, came[-1] if r > 1 else None), *(others if r == 1 else [])))
        return came, slot(None, (CHIPS - 1, residual, came[-1]))

    came_b, sums_a = overlap(pieces[b], first_b, residual_a, pair_states)
    first_step(a, residual_a, sums_a)
    residual_b = project(chunks[b], weights_bf[b], came_b)

    came_a, sums_b = overlap(second_pieces[a], slot(second_pieces[a], None), residual_b)
    first_step(b, residual_b, sums_b)
    residual_a = project(chunks[a], own_of(second_pieces[a]), came_a)

    came_b, sums_a = overlap(second_pieces[b], slot(second_pieces[b], None), residual_a)
    weights_a = last_step(a, residual_a, sums_a)
    residual_b = project(chunks[b], own_of(second_pieces[b]), came_b)

    came = slot(None, (1, residual_b, None))
    came = slot(None, (2, residual_b, came))
    weights = jnp.concatenate([weights_a, weights[:, chunks[b]]], axis=1)
    came = slot(None, (3, residual_b, came), weights)
    weights = lax.dynamic_update_slice(weights, last_step(b, residual_b, came), (0, chunks[b].start))
    outer_mean = outer[0] / lax.axis_size("island")
    momentum_new = OUTER_MOMENTUM * outer_momentum + outer_mean
    outer_update = OUTER_RATE * (outer_mean + OUTER_MOMENTUM * momentum_new)
    return (weights[None], momentum_new, outer_update)


def solution(mesh):
    return jax.shard_map(
        per_device,
        mesh=mesh,
        in_specs=(
            P("island", "fsdp", None),
            P("island", "fsdp", None),
            P("island", "fsdp"),
            P(),
            P("island", "fsdp", None),
            P("island", "fsdp", None),
            P("island", "fsdp", None),
            P("island", "fsdp", None),
            P("fsdp", None),
        ),
        out_specs=(P("island", "fsdp", None), P("fsdp", None), P("fsdp", None)),
        check_vma=False,
    )
```
